512 devices in a mesh: row: 32 (over x, z_lo), col: 16 (over z_hi, y, core).
Axes of the slice: x: 4, y: 4, z: 16 (z_hi: 2, z_lo: 8; z = z_hi * 8 + z_lo), core: 2. Of those that a mesh axis runs over, the one named last changes fastest.
Arguments:
- covariance: float32 [16384, 16384], P('row', 'col'), may hold values from -6 to 6
- left_ops: float32 [32, 3, 512, 512], P('row', None, None, 'col'), may hold values from -0.15625 to 0.15625
- right_ops: float32 [32, 3, 512, 512], P('col', None, 'row'), may hold values from -0.15625 to 0.15625
- edge_rows: float32 [2, 512, 16384], P(None, 'row', 'col'), may hold values from -6 to 6
- edge_cols: float32 [16384, 2, 512], P('row', None, 'col'), may hold values from -6 to 6
Outputs:
- forecast: float32 [16384, 16384], P('row', 'col')
The draws below stay inside these ranges and needn't reach their ends.
All inputs are finite; a program needn't handle non-finite values.
Results may differ from the reference program's by a relative error of at most 0.0003.
Values sent between devices are 32-bit elements; how exact they have to be, the bound alone decides.
No kernel may reach another device: no remote copies, remote signals or barrier semaphores. Data moves between devices by JAX's collectives and lax.ppermute only.
A program may use at most 64 MiB of HBM per device.

```python
import jax
import jax.numpy as jnp
from jax import lax

BLK = 512
NB = 32
NW = 16384


def block_levels(stream_key, dims, split, low, top_value):
    def one(axis_at, shards_of):
        draws = jax.random.uniform(jax.random.fold_in(jax.random.fold_in(stream_key, 6), axis_at), (shards_of,), jnp.float32, low / len(split), top_value / len(split))
        return jnp.repeat(jnp.exp(draws), dims[axis_at] // shards_of).reshape((-1,) + (1,) * (len(dims) - axis_at - 1))

    gain = one(*split[0])
    for cut in split[1:]:
        gain = gain * one(*cut)
    return gain


def noise(stream_key, dims, width, reach, split=(), kind=jnp.bfloat16):
    result = width * jax.random.normal(stream_key, dims, jnp.float32)
    if split:
        result = result * block_levels(stream_key, dims, split, -0.22, 0.18)
    return jnp.clip(result, -reach, reach).astype(kind)


def setup_inputs(seed: int = 0) -> dict:
    splits = jax.random.split(jax.random.key(seed), 6)
    covariance = noise(splits[0], (NW, NW), 1.0, 6.0, ((0, 32), (1, 16)), jnp.float32)
    left_ops = noise(splits[1], (NB, 3, BLK, BLK), (3 * BLK) ** -0.5, 0.15625, ((0, 32), (3, 16)), jnp.float32)
    right_ops = noise(splits[2], (NB, 3, BLK, BLK), (3 * BLK) ** -0.5, 0.15625, ((0, 16), (2, 32)), jnp.float32)
    edge_rows = noise(splits[3], (2, BLK, NW), 1.0, 6.0, ((1, 32), (2, 16)), jnp.float32)
    edge_cols = noise(splits[4], (NW, 2, BLK), 1.0, 6.0, ((0, 32), (2, 16)), jnp.float32)
    return {"covariance": covariance, "left_ops": left_ops, "right_ops": right_ops, "edge_rows": edge_rows, "edge_cols": edge_cols}


def reference(covariance, left_ops, right_ops, edge_rows, edge_cols):
    rows_ext = jnp.concatenate([edge_rows[0], covariance, edge_rows[1]], axis=0)

    def row_band(index):
        window = lax.dynamic_slice_in_dim(rows_ext, (index * BLK).astype(jnp.int32), 3 * BLK, 0)
        blocks = lax.dynamic_index_in_dim(left_ops, index.astype(jnp.int32), 0, keepdims=False)
        wide = jnp.transpose(blocks, (1, 0, 2)).reshape(BLK, 3 * BLK)
        return jnp.dot(wide, window, preferred_element_type=jnp.float32, precision=lax.Precision.HIGHEST)

    half = lax.map(row_band, jnp.arange(NB, dtype=jnp.int32)).reshape(NW, NW)
    cols_ext = jnp.concatenate([edge_cols[:, 0, :], half, edge_cols[:, 1, :]], axis=1)

    def col_band(index):
        window = lax.dynamic_slice_in_dim(cols_ext, (index * BLK).astype(jnp.int32), 3 * BLK, 1)
        blocks = lax.dynamic_index_in_dim(right_ops, index.astype(jnp.int32), 0, keepdims=False)
        wide = jnp.transpose(blocks, (1, 0, 2)).reshape(BLK, 3 * BLK)
        return jnp.dot(window, wide.T, preferred_element_type=jnp.float32, precision=lax.Precision.HIGHEST)

    bands = lax.map(col_band, jnp.arange(NB, dtype=jnp.int32))
    return jnp.transpose(bands, (1, 0, 2)).reshape(NW, NW)
```

```python
import jax
import jax.numpy as jnp
from jax import lax
from jax.sharding import PartitionSpec as P

NX, NZ, NH, NY, NC = 4, 8, 2, 4, 2
HIGH = lax.Precision.HIGH
AXES = ("row", "col")


def moved(array, target):
    pairs = []
    for x in range(NX):
        for z in range(NZ):
            for h in range(NH):
                for y in range(NY):
                    for c in range(NC):
                        to = target(x, z, h, y, c)
                        if to is not None:
                            pairs.append((flat(x, z, h, y, c), flat(*to)))
    return lax.ppermute(array, AXES, pairs)


def flat(x, z, h, y, c):
    return (((x * NZ + z) * NH + h) * NY + y) * NC + c


def row_step(d):
    def target(x, z, h, y, c):
        r = x * NZ + z + d
        return (r // NZ, r % NZ, h, y, c) if 0 <= r < NX * NZ else None

    return target


def col_step(d):
    def target(x, z, h, y, c):
        k = (h * NY + y) * NC + c + d
        return (x, z, k // 8, k % 8 // 2, k % 2) if 0 <= k < 16 else None

    return target


def x_step(d):
    return lambda x, z, h, y, c: ((x + d) % NX, z, h, y, c)


def y_step(d):
    return lambda x, z, h, y, c: (x, z, h, (y + d) % NY, c)


def z_swap(bit):
    return lambda x, z, h, y, c: (x, z ^ bit, h, y, c)


def h_swap(x, z, h, y, c):
    return (x, z, 1 - h, y, c)


def core_swap(x, z, h, y, c):
    return (x, z, h, y, 1 - c)


def dot(a, b, dims):
    return lax.dot_general(
        a, b, (dims, ((), ())), precision=HIGH, preferred_element_type=jnp.float32
    )


def gather_left(left, edge, h, y, c):
    own = jnp.concatenate([left, jnp.where(h == 0, edge[1], edge[0])], axis=0)
    keep = jnp.concatenate([left, jnp.where(h == 0, edge[0], edge[1])], axis=0)
    other = moved(own, h_swap)
    pair = jnp.stack([jnp.where(h == 0, keep, other), jnp.where(h == 0, other, keep)])
    below = moved(pair, y_step(1))
    above = moved(pair, y_step(-1))
    across = moved(pair, y_step(2))
    ring = jnp.stack([pair, above, across, below])
    ring = jnp.concatenate([ring, ring])
    ring = lax.dynamic_slice_in_dim(ring, NY - y, NY, axis=0)
    mate = moved(ring, core_swap)
    both = jnp.stack([jnp.where(c == 0, ring, mate), jnp.where(c == 0, mate, ring)])
    full = both.reshape(NC, NY, NH, 4, 32, 512).transpose(3, 2, 1, 0, 4, 5)
    full = full.reshape(4, 512, 512)
    return full[:3], full[3]


def gather_right(right, x, z):
    b2, b1, b0 = z // 4, z // 2 % 2, z % 2
    zero = jnp.int32(0)
    full = jnp.zeros((2, 3, NX, 2, 2, 2, 16, 512), jnp.float32)

    def put(full, block, where):
        return lax.dynamic_update_slice(full, block, (zero, zero, *where, zero, zero))

    def put_all(full, block, where):
        full = put(full, block, (x, *where))
        for d in (1, -1, 2):
            full = put(full, moved(block, x_step(d)), ((x + NX - d) % NX, *where))
        return full

    own = right.reshape(2, 3, 1, 1, 1, 1, 16, 512)
    far = moved(own, z_swap(4))
    pair = jnp.concatenate([jnp.where(b2 == 0, own, far), jnp.where(b2 == 0, far, own)], axis=3)
    mid = moved(pair, z_swap(2))
    quad = jnp.concatenate([jnp.where(b1 == 0, pair, mid), jnp.where(b1 == 0, mid, pair)], axis=4)
    near = moved(quad, z_swap(1))
    full = put_all(full, pair, (zero, b1, b0))
    full = put_all(full, mid, (zero, 1 - b1, b0))
    full = put_all(full, near, (zero, zero, 1 - b0))
    return full.reshape(2, 3, 512, 512)


def gather_rows(edge, z):
    def toward(bit, size):
        def target(x, z, h, y, c):
            if bit == 4:
                return (x, z ^ 4, h, y, c)
            low = z < 4
            rest = z if low else 7 - z
            if rest < 2 * bit and rest >= bit:
                return (x, z - bit if low else z + bit, h, y, c)
            return None

        return target

    low = z < 4
    keep = jnp.where(low, edge[0], edge[1])[None]
    send = jnp.where(low, edge[1], edge[0])[None]
    got = moved(send, toward(4, 1))
    block = jnp.concatenate([jnp.where(low, keep, got), jnp.where(low, got, keep)])
    block = block.reshape(2, 1, 1, 16, 1024)
    got = moved(block, toward(2, 2))
    block = jnp.concatenate([jnp.where(low, block, got), jnp.where(low, got, block)], axis=1)
    got = moved(block, toward(1, 4))
    block = jnp.concatenate([jnp.where(low, block, got), jnp.where(low, got, block)], axis=2)
    block = block.reshape(1, 128, 1024)

    def x_one(x, z, h, y, c):
        if z == 0:
            return (x - 1, z, h, y, c) if x % 2 == 1 else None
        if z == NZ - 1:
            return (x + 1, z, h, y, c) if x % 2 == 0 else None
        return None

    def x_two(x, z, h, y, c):
        if z == 0:
            return (0, z, h, y, c) if x == 2 else None
        if z == NZ - 1:
            return (3, z, h, y, c) if x == 1 else None
        return None

    got = moved(block, x_one)
    block = jnp.concatenate([jnp.where(low, block, got), jnp.where(low, got, block)])
    got = moved(block, x_two)
    block = jnp.concatenate([jnp.where(low, block, got), jnp.where(low, got, block)])
    return block.reshape(512, 1024)


def on_device(covariance, left_ops, right_ops, edge_rows, edge_cols):
    row, col = lax.axis_index("row"), lax.axis_index("col")
    x, z = row // NZ, row % NZ
    h, y, c = col // 8, col // 2 % NY, col % NC
    size = covariance.shape[0]

    left = left_ops[0].transpose(0, 2, 1).reshape(96, 512)
    edge = edge_cols.transpose(1, 2, 0)
    left_full, side = gather_left(left, edge, h, y, c)

    bands = [covariance[:, :size], covariance[:, size:]]
    upper = [moved(band, row_step(1)) for band in bands]
    lower = [moved(band, row_step(-1)) for band in bands]
    outside = gather_rows(edge_rows, z)
    right_full = gather_right(right_ops, x, z)

    half = []
    for k, band in enumerate(bands):
        out = outside[:, k * size : (k + 1) * size]
        top = jnp.where(row == 0, out, upper[k])
        bottom = jnp.where(row == NX * NZ - 1, out, lower[k])
        part = dot(left_full[1], band, ((0,), (0,)))
        part = part + dot(left_full[0], top, ((0,), (0,)))
        half.append(part + dot(left_full[2], bottom, ((0,), (0,))))

    before = moved(half[1], col_step(1))
    after = moved(half[0], col_step(-1))
    before = jnp.where(col == 0, side.T, before)
    after = jnp.where(col == 15, side.T, after)
    line = [before, half[0], half[1], after]
    result = []
    for j in range(2):
        part = dot(half[0], right_full[j, 1 - j], ((1,), (1,)))
        part = part + dot(half[1], right_full[j, 2 - j], ((1,), (1,)))
        part = part + dot(line[3 * j], right_full[j, 2 * j], ((1,), (1,)))
        result.append(part)
    return jnp.concatenate(result, axis=1)


def solution(mesh):
    return jax.shard_map(
        on_device,
        mesh=mesh,
        in_specs=(
            P("row", "col"),
            P("row", None, None, "col"),
            P("col", None, "row", None),
            P(None, "row", "col"),
            P("row", None, "col"),
        ),
        out_specs=P("row", "col"),
        check_vma=False,
    )
```

```python
import jax
import jax.numpy as jnp
from jax import lax
from jax.experimental import pallas as pl
from jax.experimental.pallas import tpu as pltpu
from jax.sharding import PartitionSpec as P

NX, NZ, NH, NY, NC = 4, 8, 2, 4, 2
AXES = ("row", "col")


def moved(array, target):
    pairs = []
    for x in range(NX):
        for z in range(NZ):
            for h in range(NH):
                for y in range(NY):
                    for c in range(NC):
                        to = target(x, z, h, y, c)
                        if to is not None:
                            pairs.append((flat(x, z, h, y, c), flat(*to)))
    return lax.ppermute(array, AXES, pairs)


def flat(x, z, h, y, c):
    return (((x * NZ + z) * NH + h) * NY + y) * NC + c


def row_step(d):
    def target(x, z, h, y, c):
        r = x * NZ + z + d
        return (r // NZ, r % NZ, h, y, c) if 0 <= r < NX * NZ else None

    return target


def col_step(d):
    def target(x, z, h, y, c):
        k = (h * NY + y) * NC + c + d
        return (x, z, k // 8, k % 8 // 2, k % 2) if 0 <= k < 16 else None

    return target


def x_step(d):
    return lambda x, z, h, y, c: ((x + d) % NX, z, h, y, c)


def y_step(d):
    return lambda x, z, h, y, c: (x, z, h, (y + d) % NY, c)


def z_swap(bit):
    return lambda x, z, h, y, c: (x, z ^ bit, h, y, c)


def rows_of(band):
    return moved(band, row_step(1)), moved(band, row_step(-1))


def h_swap(x, z, h, y, c):
    return (x, z, 1 - h, y, c)


def core_swap(x, z, h, y, c):
    return (x, z, h, y, 1 - c)


def after(array, *others):
    return lax.optimization_barrier((array, *others))[0]


def left_first(left, edge, h):
    other = moved(jnp.concatenate([left, jnp.where(h == 0, edge[1], edge[0])], axis=0), h_swap)
    own = jnp.concatenate([left, jnp.where(h == 0, edge[0], edge[1])], axis=0)
    return jnp.stack([own, other])


def left_second(pair, place, *gate):
    pieces = [pair, moved(pair, y_step(-1)), moved(pair, y_step(2)), moved(pair, y_step(1))]
    mates = [moved(after(piece, *gate), core_swap) for piece in pieces]
    return assembled(place, pieces + mates)


def assemble_kernel(place_ref, *refs):
    pieces, (high_ref, low_ref, side_ref) = refs[:8], refs[8:]
    h, y, c = place_ref[0], place_ref[1], place_ref[2]
    for k, piece in enumerate(pieces):
        core = c if k < 4 else 1 - c
        line = lax.rem(y + k % 4, NY)
        for far in range(2):
            side = h if far == 0 else 1 - h
            at = pl.multiple_of(((side * NY + line) * NC + core) * 32, 32)
            for m in range(3):
                high, low = split(piece[far, pl.ds(m * 32, 32), :])
                high_ref[m, pl.ds(at, 32), :] = high
                low_ref[m, pl.ds(at, 32), :] = low
            side_ref[pl.ds(at, 32), :] = piece[far, pl.ds(96, 32), :]


def assembled(place, pieces):
    size = pieces[0].shape[2]
    half = jax.ShapeDtypeStruct((3, size, size), jnp.bfloat16)
    return pl.pallas_call(
        assemble_kernel,
        out_shape=(half, half, jax.ShapeDtypeStruct((size, size), jnp.float32)),
        in_specs=[pl.BlockSpec(memory_space=pltpu.SMEM)]
        + [pl.BlockSpec(memory_space=pltpu.VMEM)] * 8,
        out_specs=(pl.BlockSpec(memory_space=pltpu.VMEM),) * 3,
        compiler_params=PARAMS,
        cost_estimate=pl.CostEstimate(
            flops=0, bytes_accessed=32 * size**2, transcendentals=0
        ),
    )(place, *pieces)


def half_kernel(place_ref, band_ref, outside_ref, high_ref, low_ref, *refs):
    (*parts, out_ref) = refs
    upper, lower = (
        jnp.concatenate([ref[...] for ref in parts[k::2]], axis=1) for k in range(2)
    )
    outside = outside_ref[...]
    blocks = (
        jnp.where(place_ref[1] == 0, outside, upper),
        band_ref[...],
        jnp.where(place_ref[1] == NX * NZ - 1, outside, lower),
    )
    dims = (((0,), (0,)), ((), ()))
    total = None
    for m in (1, 0, 2):
        high, low = split(blocks[m])
        for left, block in ((high_ref, low), (low_ref, high), (high_ref, high)):
            part = lax.dot_general(left[m], block, dims, preferred_element_type=jnp.float32)
            total = part if total is None else total + part
    out_ref[...] = total


def half_products(inner, place, covariance, outside, high, low, parts):
    parts = [piece for part in parts for piece in part]
    size = covariance.shape[0]
    column = pl.BlockSpec((size, size), lambda i, place: (0, place[0] ^ inner))
    return pl.pallas_call(
        half_kernel,
        out_shape=jax.ShapeDtypeStruct((size, size), jnp.float32),
        grid_spec=pltpu.PrefetchScalarGridSpec(
            num_scalar_prefetch=1,
            grid=(1,),
            in_specs=[column, column]
            + [whole(3, size, size)] * 2
            + [whole(*piece.shape) for piece in parts],
            out_specs=whole(size, size),
        ),
        compiler_params=PARAMS,
        cost_estimate=pl.CostEstimate(
            flops=18 * size**3, bytes_accessed=32 * size**2, transcendentals=0
        ),
    )(place, covariance, outside, high, low, *parts)


def gather_line(right):
    lines = [[x * NZ + z for z in range(NZ)] for x in range(NX)]
    return lax.all_gather(right, "row", axis_index_groups=lines, axis=2, tiled=True)


def gather_ring(line):
    rings = [[x * NZ + z for x in range(NX)] for z in range(NZ)]
    return lax.all_gather(line, "row", axis_index_groups=rings, axis=2, tiled=True)


def outward(x, z, h, y, c):
    return col_step(1 if c == 1 else -1)(x, z, h, y, c)


def toward(bit):
    def target(x, z, h, y, c):
        if bit == 4:
            return (x, z ^ 4, h, y, c)
        low = z < 4
        rest = z if low else NZ - 1 - z
        if bit <= rest < 2 * bit:
            return (x, z - bit if low else z + bit, h, y, c)
        return None

    return target


def rows_first(edge, z, gate):
    low = z < 4
    keep = jnp.where(low, edge[0], edge[1])[None]
    send = jnp.where(low, edge[1], edge[0])[None]
    got = moved(send, toward(4))
    block = jnp.concatenate([jnp.where(low, keep, got), jnp.where(low, got, keep)])
    block = block.reshape(2, 1, 1, 16, 1024)
    got = moved(after(block, gate), toward(2))
    block = jnp.concatenate([jnp.where(low, block, got), jnp.where(low, got, block)], axis=1)
    got = moved(block, toward(1))
    block = jnp.concatenate([jnp.where(low, block, got), jnp.where(low, got, block)], axis=2)
    return block.reshape(1, 128, 1024)


def rows_second(block, z, *gate):
    low = z < 4

    def x_one(x, z, h, y, c):
        if z == 0:
            return (x - 1, z, h, y, c) if x % 2 == 1 else None
        if z == NZ - 1:
            return (x + 1, z, h, y, c) if x % 2 == 0 else None
        return None

    def x_two(x, z, h, y, c):
        if z == 0:
            return (0, z, h, y, c) if x == 2 else None
        if z == NZ - 1:
            return (3, z, h, y, c) if x == 1 else None
        return None

    got = moved(block, x_one)
    block = jnp.concatenate([jnp.where(low, block, got), jnp.where(low, got, block)])
    got = moved(after(block, *gate), x_two)
    block = jnp.concatenate([jnp.where(low, block, got), jnp.where(low, got, block)])
    return block.reshape(512, 1024)


def on_device(covariance, left_ops, right_ops, edge_rows, edge_cols):
    row, col = lax.axis_index("row"), lax.axis_index("col")
    x, z = row // NZ, row % NZ
    h, y, c = col // 8, col // 2 % NY, col % NC
    size = covariance.shape[0]

    def band_of(array, inner):
        return lax.dynamic_slice_in_dim(array, (c ^ inner) * size, size, axis=1)

    line = gather_line(right_ops)
    left = left_ops[0].transpose(0, 2, 1).reshape(96, size)
    pair = left_first(left, edge_cols.transpose(1, 2, 0), h)
    shares = rows_first(edge_rows, z, pair)
    lead = size // 4
    band = after(band_of(covariance, 0), pair, shares)
    outer = [rows_of(part) for part in (band[:, :lead], band[:, lead:])]
    high, low, side = left_second(pair, jnp.stack([h, y, c]), *outer[0])
    outside = rows_second(shares, z, *outer[0])
    line, band = lax.optimization_barrier(
        (line, band_of(covariance, 1), *outer[0], *outer[1], side, outside)
    )[:2]
    right_full = gather_ring(line)
    inner = [rows_of(band)]
    place = jnp.stack([c, row])
    half_outer = half_products(0, place, covariance, outside, high, low, outer)
    cross = moved(half_outer, outward)
    half_inner = half_products(1, place, covariance, outside, high, low, inner)
    sibling = moved(half_inner, core_swap)
    core = jnp.stack([c, jnp.where((col == 0) | (col == 15), 1, 0)])
    sums = first_products(core, half_outer, cross, side, right_full)
    return last_products(core, half_inner, sibling, right_full, *sums)


def split(array):
    high = array.astype(jnp.bfloat16)
    return high, (array - high.astype(jnp.float32)).astype(jnp.bfloat16)


def times(a, b):
    dims = (((1,), (1,)), ((), ()))
    total = lax.dot_general(a[0], b[1], dims, preferred_element_type=jnp.float32)
    total += lax.dot_general(a[1], b[0], dims, preferred_element_type=jnp.float32)
    return total + lax.dot_general(a[0], b[0], dims, preferred_element_type=jnp.float32)


def first_kernel(
    c_ref, near_ref, cross_ref, side_ref, r0_ref, r1_ref, r2_ref, outer_ref, inner_ref, held
):
    held[...] = cross_ref[...]

    @pl.when(c_ref[1] == 1)
    def _():
        held[...] = side_ref[...].T

    near, cross = split(near_ref[...]), split(held[...])
    inner_ref[...] = times(near, split(r2_ref[...]))
    outer_ref[...] = times(near, split(r1_ref[...])) + times(cross, split(r0_ref[...]))


def last_kernel(c_ref, near_ref, sibling_ref, r0_ref, r1_ref, r2_ref, outer_ref, inner_ref, out_ref):
    c, size = c_ref[0], near_ref.shape[0]
    near = split(near_ref[...])
    at = pl.multiple_of(c * size, 128)
    out_ref[:, pl.ds(at, size)] = outer_ref[...] + times(near, split(r2_ref[...]))
    at = pl.multiple_of((1 - c) * size, 128)
    total = inner_ref[...] + times(near, split(r1_ref[...]))
    out_ref[:, pl.ds(at, size)] = total + times(split(sibling_ref[...]), split(r0_ref[...]))


def whole(*shape):
    return pl.BlockSpec(shape, lambda i, c: (0,) * len(shape))


def block_at(place, size):
    return pl.BlockSpec((None, None, size, size), lambda i, c: (*place(c[0]), 0, 0))


PARAMS = pltpu.CompilerParams(vmem_limit_bytes=48 * 2**20)


def first_products(c, near, cross, side, right):
    size = near.shape[0]
    square = jax.ShapeDtypeStruct((size, size), jnp.float32)
    return pl.pallas_call(
        first_kernel,
        out_shape=(square, square),
        grid_spec=pltpu.PrefetchScalarGridSpec(
            num_scalar_prefetch=1,
            grid=(1,),
            in_specs=[whole(size, size)] * 3
            + [
                block_at(lambda c: (c, 2 * c), size),
                block_at(lambda c: (c, 1), size),
                block_at(lambda c: (1 - c, 2 * c), size),
            ],
            out_specs=(whole(size, size), whole(size, size)),
            scratch_shapes=[pltpu.VMEM((size, size), jnp.float32)],
        ),
        compiler_params=PARAMS,
        cost_estimate=pl.CostEstimate(
            flops=18 * size**3, bytes_accessed=28 * size**2, transcendentals=0
        ),
    )(c, near, cross, side, right, right, right)


def last_products(c, near, sibling, right, outer, inner):
    size = near.shape[0]
    return pl.pallas_call(
        last_kernel,
        out_shape=jax.ShapeDtypeStruct((size, 2 * size), jnp.float32),
        grid_spec=pltpu.PrefetchScalarGridSpec(
            num_scalar_prefetch=1,
            grid=(1,),
            in_specs=[whole(size, size)] * 2
            + [
                block_at(lambda c: (1 - c, 2 - 2 * c), size),
                block_at(lambda c: (1 - c, 1), size),
                block_at(lambda c: (c, 2 - 2 * c), size),
            ]
            + [whole(size, size)] * 2,
            out_specs=whole(size, 2 * size),
        ),
        compiler_params=PARAMS,
        cost_estimate=pl.CostEstimate(
            flops=18 * size**3, bytes_accessed=36 * size**2, transcendentals=0
        ),
    )(c, near, sibling, right, right, right, outer, inner)


def solution(mesh):
    return jax.shard_map(
        on_device,
        mesh=mesh,
        in_specs=(
            P("row", "col"),
            P("row", None, None, "col"),
            P("col", None, "row", None),
            P(None, "row", "col"),
            P("row", None, "col"),
        ),
        out_specs=P("row", "col"),
        check_vma=False,
    )
```

```python
import jax
import jax.numpy as jnp
from jax import lax
from jax.experimental import pallas as pl
from jax.experimental.pallas import tpu as pltpu
from jax.sharding import PartitionSpec as P

NX, NZ, NH, NY, NC = 4, 8, 2, 4, 2
AXES = ("row", "col")


def moved(array, target):
    pairs = []
    for x in range(NX):
        for z in range(NZ):
            for h in range(NH):
                for y in range(NY):
                    for c in range(NC):
                        to = target(x, z, h, y, c)
                        if to is not None:
                            pairs.append((flat(x, z, h, y, c), flat(*to)))
    return lax.ppermute(array, AXES, pairs)


def flat(x, z, h, y, c):
    return (((x * NZ + z) * NH + h) * NY + y) * NC + c


def row_step(d):
    def target(x, z, h, y, c):
        r = x * NZ + z + d
        return (r // NZ, r % NZ, h, y, c) if 0 <= r < NX * NZ else None

    return target


def col_step(d):
    def target(x, z, h, y, c):
        k = (h * NY + y) * NC + c + d
        return (x, z, k // 8, k % 8 // 2, k % 2) if 0 <= k < 16 else None

    return target


def x_step(d):
    return lambda x, z, h, y, c: ((x + d) % NX, z, h, y, c)


def y_step(d):
    return lambda x, z, h, y, c: (x, z, h, (y + d) % NY, c)


def z_swap(bit):
    return lambda x, z, h, y, c: (x, z ^ bit, h, y, c)


def rows_of(band):
    return moved(band, row_step(1)), moved(band, row_step(-1))


def h_swap(x, z, h, y, c):
    return (x, z, 1 - h, y, c)


def core_swap(x, z, h, y, c):
    return (x, z, h, y, 1 - c)


def after(array, *others):
    return lax.optimization_barrier((array, *others))[0]


def left_first(left, edge, h):
    other = moved(jnp.concatenate([left, jnp.where(h == 0, edge[1], edge[0])], axis=0), h_swap)
    own = jnp.concatenate([left, jnp.where(h == 0, edge[0], edge[1])], axis=0)
    return jnp.stack([own, other])


def along_y(pair):
    return [pair] + [moved(pair, y_step(d)) for d in (-1, 2, 1)]


def assemble_kernel(place_ref, own_ref, mate_ref, high_ref, low_ref, side_ref):
    h, y, c = place_ref[0], place_ref[1], place_ref[2]
    for ref, core in ((own_ref, c), (mate_ref, 1 - c)):
        for d in range(NY):
            line = lax.rem(y + d, NY)
            for far in range(2):
                side = h if far == 0 else 1 - h
                at = pl.multiple_of(((side * NY + line) * NC + core) * 32, 32)
                for m in range(3):
                    high, low = split(ref[d, far, pl.ds(m * 32, 32), :])
                    high_ref[m, pl.ds(at, 32), :] = high
                    low_ref[m, pl.ds(at, 32), :] = low
                side_ref[pl.ds(at, 32), :] = ref[d, far, pl.ds(96, 32), :]


def assembled(place, own, mate):
    size = own.shape[3]
    half = jax.ShapeDtypeStruct((3, size, size), jnp.bfloat16)
    return pl.pallas_call(
        assemble_kernel,
        out_shape=(half, half, jax.ShapeDtypeStruct((size, size), jnp.float32)),
        in_specs=[pl.BlockSpec(memory_space=pltpu.SMEM)]
        + [pl.BlockSpec(memory_space=pltpu.VMEM)] * 2,
        out_specs=(pl.BlockSpec(memory_space=pltpu.VMEM),) * 3,
        compiler_params=PARAMS,
        cost_estimate=pl.CostEstimate(
            flops=0, bytes_accessed=32 * size**2, transcendentals=0
        ),
    )(place, own, mate)


def half_kernel(place_ref, band_ref, high_ref, low_ref, *refs):
    edges, parts, (out_ref, top, bottom) = refs[:NX], refs[NX:-3], refs[-3:]
    at = 0
    for upper_ref, lower_ref in zip(parts[::2], parts[1::2]):
        width = upper_ref.shape[1]
        top[:, at : at + width] = upper_ref[...]
        bottom[:, at : at + width] = lower_ref[...]
        at += width

    def fill(ref, mirror):
        for k, edge in enumerate(edges):
            for d in range(4):
                for far in range(2):
                    x, z = (NX - 1 - k, 3 - d) if mirror else (k, d)
                    at = (x * NZ + far * 4 + z) * 16
                    ref[at : at + 16, :] = edge[(d * 2 + far) * 16 : (d * 2 + far + 1) * 16, :]

    @pl.when(place_ref[1] == 0)
    def _():
        fill(top, False)

    @pl.when(place_ref[1] == NX * NZ - 1)
    def _():
        fill(bottom, True)

    dims = (((0,), (0,)), ((), ()))
    total = None
    for m, ref in ((1, band_ref), (0, top), (2, bottom)):
        high, low = split(ref[...])
        for left, block in ((high_ref, low), (low_ref, high), (high_ref, high)):
            part = lax.dot_general(left[m], block, dims, preferred_element_type=jnp.float32)
            total = part if total is None else total + part
    out_ref[...] = total


def half_products(inner, place, covariance, high, low, edges, parts):
    size = covariance.shape[0]
    parts = [piece for part in parts for piece in part]

    def column(rows):
        return pl.BlockSpec((rows, size), lambda i, place: (0, place[0] ^ inner))

    return pl.pallas_call(
        half_kernel,
        out_shape=jax.ShapeDtypeStruct((size, size), jnp.float32),
        grid_spec=pltpu.PrefetchScalarGridSpec(
            num_scalar_prefetch=1,
            grid=(1,),
            in_specs=[column(size)]
            + [whole(3, size, size)] * 2
            + [column(size // NX)] * NX
            + [whole(*piece.shape) for piece in parts],
            out_specs=whole(size, size),
            scratch_shapes=[pltpu.VMEM((size, size), jnp.float32)] * 2,
        ),
        compiler_params=PARAMS,
        cost_estimate=pl.CostEstimate(
            flops=18 * size**3, bytes_accessed=32 * size**2, transcendentals=0
        ),
    )(place, covariance, high, low, *edges, *parts)


def gather_line(right):
    lines = [[x * NZ + z for z in range(NZ)] for x in range(NX)]
    return lax.all_gather(right, "row", axis_index_groups=lines, axis=2, tiled=True)


def gather_ring(line):
    rings = [[x * NZ + z for x in range(NX)] for z in range(NZ)]
    return lax.all_gather(line, "row", axis_index_groups=rings, axis=2, tiled=True)


def outward(x, z, h, y, c):
    return col_step(1 if c == 1 else -1)(x, z, h, y, c)


def toward(distance):
    def target(x, z, h, y, c):
        if z == distance:
            return (x, 0, h, y, c)
        if NZ - 1 - z == distance:
            return (x, NZ - 1, h, y, c)
        return None

    return target


def across(distance):
    def target(x, z, h, y, c):
        if z == 0 and x == distance:
            return (0, z, h, y, c)
        if z == NZ - 1 and NX - 1 - x == distance:
            return (NX - 1, z, h, y, c)
        return None

    return target


def rows_first(edge, z):
    low = z < 4
    keep = jnp.where(low, edge[0], edge[1])
    got = moved(jnp.where(low, edge[1], edge[0]), z_swap(4))
    return jnp.concatenate([jnp.where(low, keep, got), jnp.where(low, got, keep)])


def rows_second(share, gate):
    sent = after(share, *gate)
    return jnp.concatenate([share] + [moved(sent, toward(d)) for d in (1, 2, 3)])


def rows_third(share, gate):
    sent = after(share, *gate)
    return [share] + [moved(sent, across(d)) for d in (1, 2, 3)]


def on_device(covariance, left_ops, right_ops, edge_rows, edge_cols):
    row, col = lax.axis_index("row"), lax.axis_index("col")
    x, z = row // NZ, row % NZ
    h, y, c = col // 8, col // 2 % NY, col % NC
    size = covariance.shape[0]

    def band_of(array, inner):
        return lax.dynamic_slice_in_dim(array, (c ^ inner) * size, size, axis=1)

    line = gather_line(right_ops)
    left = left_ops[0].transpose(0, 2, 1).reshape(96, size)
    pair = left_first(left, edge_cols.transpose(1, 2, 0), h)
    share = rows_first(edge_rows, z)
    band = band_of(covariance, 0)
    outer = [rows_of(band[:, : size // 2])]
    pieces = along_y(after(pair, share, *outer[0]))
    outer.append(rows_of(after(band[:, size // 2 :], share, pair)))
    share = rows_second(share, outer[1])
    right_full = gather_ring(after(line, *outer[1], *pieces))
    pieces = jnp.stack(pieces)
    mates = moved(after(pieces, *outer[1]), core_swap)
    band = after(band_of(covariance, 1), *outer[1])
    inner = [rows_of(band)]
    edges = rows_third(share, outer[0])
    high, low, side = assembled(jnp.stack([h, y, c]), pieces, mates)
    place = jnp.stack([c, row])
    half_outer = half_products(0, place, covariance, high, low, edges, outer)
    cross = moved(half_outer, outward)
    half_inner = half_products(1, place, covariance, high, low, edges, inner)
    sibling = moved(half_inner, core_swap)
    core = jnp.stack([c, jnp.where((col == 0) | (col == 15), 1, 0)])
    sums = first_products(core, half_outer, cross, side, right_full)
    return last_products(core, half_inner, sibling, right_full, *sums)


def split(array):
    high = array.astype(jnp.bfloat16)
    return high, (array - high.astype(jnp.float32)).astype(jnp.bfloat16)


def times(a, b):
    dims = (((1,), (1,)), ((), ()))
    total = lax.dot_general(a[0], b[1], dims, preferred_element_type=jnp.float32)
    total += lax.dot_general(a[1], b[0], dims, preferred_element_type=jnp.float32)
    return total + lax.dot_general(a[0], b[0], dims, preferred_element_type=jnp.float32)


def first_kernel(
    c_ref, near_ref, cross_ref, side_ref, r0_ref, r1_ref, r2_ref, outer_ref, inner_ref, held
):
    held[...] = cross_ref[...]

    @pl.when(c_ref[1] == 1)
    def _():
        held[...] = side_ref[...].T

    near, cross = split(near_ref[...]), split(held[...])
    inner_ref[...] = times(near, split(r2_ref[...]))
    outer_ref[...] = times(near, split(r1_ref[...])) + times(cross, split(r0_ref[...]))


def last_kernel(c_ref, near_ref, sibling_ref, r0_ref, r1_ref, r2_ref, outer_ref, inner_ref, out_ref):
    c, size = c_ref[0], near_ref.shape[0]
    near = split(near_ref[...])
    at = pl.multiple_of(c * size, 128)
    out_ref[:, pl.ds(at, size)] = outer_ref[...] + times(near, split(r2_ref[...]))
    at = pl.multiple_of((1 - c) * size, 128)
    total = inner_ref[...] + times(near, split(r1_ref[...]))
    out_ref[:, pl.ds(at, size)] = total + times(split(sibling_ref[...]), split(r0_ref[...]))


def whole(*shape):
    return pl.BlockSpec(shape, lambda i, c: (0,) * len(shape))


def block_at(place, size):
    return pl.BlockSpec((None, None, size, size), lambda i, c: (*place(c[0]), 0, 0))


PARAMS = pltpu.CompilerParams(vmem_limit_bytes=48 * 2**20)


def first_products(c, near, cross, side, right):
    size = near.shape[0]
    square = jax.ShapeDtypeStruct((size, size), jnp.float32)
    return pl.pallas_call(
        first_kernel,
        out_shape=(square, square),
        grid_spec=pltpu.PrefetchScalarGridSpec(
            num_scalar_prefetch=1,
            grid=(1,),
            in_specs=[whole(size, size)] * 3
            + [
                block_at(lambda c: (c, 2 * c), size),
                block_at(lambda c: (c, 1), size),
                block_at(lambda c: (1 - c, 2 * c), size),
            ],
            out_specs=(whole(size, size), whole(size, size)),
            scratch_shapes=[pltpu.VMEM((size, size), jnp.float32)],
        ),
        compiler_params=PARAMS,
        cost_estimate=pl.CostEstimate(
            flops=18 * size**3, bytes_accessed=28 * size**2, transcendentals=0
        ),
    )(c, near, cross, side, right, right, right)


def last_products(c, near, sibling, right, outer, inner):
    size = near.shape[0]
    return pl.pallas_call(
        last_kernel,
        out_shape=jax.ShapeDtypeStruct((size, 2 * size), jnp.float32),
        grid_spec=pltpu.PrefetchScalarGridSpec(
            num_scalar_prefetch=1,
            grid=(1,),
            in_specs=[whole(size, size)] * 2
            + [
                block_at(lambda c: (1 - c, 2 - 2 * c), size),
                block_at(lambda c: (1 - c, 1), size),
                block_at(lambda c: (c, 2 - 2 * c), size),
            ]
            + [whole(size, size)] * 2,
            out_specs=whole(size, 2 * size),
        ),
        compiler_params=PARAMS,
        cost_estimate=pl.CostEstimate(
            flops=18 * size**3, bytes_accessed=36 * size**2, transcendentals=0
        ),
    )(c, near, sibling, right, right, right, outer, inner)


def solution(mesh):
    return jax.shard_map(
        on_device,
        mesh=mesh,
        in_specs=(
            P("row", "col"),
            P("row", None, None, "col"),
            P("col", None, "row", None),
            P(None, "row", "col"),
            P("row", None, "col"),
        ),
        out_specs=P("row", "col"),
        check_vma=False,
    )
```

```python
import jax
import jax.numpy as jnp
from jax import lax
from jax.experimental import pallas as pl
from jax.experimental.pallas import tpu as pltpu
from jax.sharding import PartitionSpec as P

NX, NZ, NH, NY, NC = 4, 8, 2, 4, 2
AXES = ("row", "col")


def moved(array, target):
    pairs = []
    for x in range(NX):
        for z in range(NZ):
            for h in range(NH):
                for y in range(NY):
                    for c in range(NC):
                        to = target(x, z, h, y, c)
                        if to is not None:
                            pairs.append((flat(x, z, h, y, c), flat(*to)))
    return lax.ppermute(array, AXES, pairs)


def flat(x, z, h, y, c):
    return (((x * NZ + z) * NH + h) * NY + y) * NC + c


def row_step(d):
    def target(x, z, h, y, c):
        r = x * NZ + z + d
        return (r // NZ, r % NZ, h, y, c) if 0 <= r < NX * NZ else None

    return target


def col_step(d):
    def target(x, z, h, y, c):
        k = (h * NY + y) * NC + c + d
        return (x, z, k // 8, k % 8 // 2, k % 2) if 0 <= k < 16 else None

    return target


def x_step(d):
    return lambda x, z, h, y, c: ((x + d) % NX, z, h, y, c)


def y_step(d):
    return lambda x, z, h, y, c: (x, z, h, (y + d) % NY, c)


def z_swap(bit):
    return lambda x, z, h, y, c: (x, z ^ bit, h, y, c)


def rows_of(band):
    return moved(band, row_step(1)), moved(band, row_step(-1))


def h_swap(x, z, h, y, c):
    return (x, z, 1 - h, y, c)


def core_swap(x, z, h, y, c):
    return (x, z, h, y, 1 - c)


def after(array, *others):
    return lax.optimization_barrier((array, *others))[0]


def left_first(left, edge, h):
    other = moved(jnp.concatenate([left, jnp.where(h == 0, edge[1], edge[0])], axis=0), h_swap)
    own = jnp.concatenate([left, jnp.where(h == 0, edge[0], edge[1])], axis=0)
    return jnp.stack([own, other])


def along_y(pair):
    return [pair] + [moved(pair, y_step(d)) for d in (-1, 2, 1)]


def assemble_kernel(place_ref, own_ref, mate_ref, high_ref, low_ref, side_ref):
    h, y, c = place_ref[0], place_ref[1], place_ref[2]
    for ref, core in ((own_ref, c), (mate_ref, 1 - c)):
        for d in range(NY):
            line = lax.rem(y + d, NY)
            for far in range(2):
                side = h if far == 0 else 1 - h
                at = pl.multiple_of(((side * NY + line) * NC + core) * 32, 32)
                for m in range(3):
                    high, low = split(ref[d, far, pl.ds(m * 32, 32), :])
                    high_ref[m, pl.ds(at, 32), :] = high
                    low_ref[m, pl.ds(at, 32), :] = low
                side_ref[pl.ds(at, 32), :] = ref[d, far, pl.ds(96, 32), :]


def assembled(place, own, mate):
    size = own.shape[3]
    half = jax.ShapeDtypeStruct((3, size, size), jnp.bfloat16)
    return pl.pallas_call(
        assemble_kernel,
        out_shape=(half, half, jax.ShapeDtypeStruct((size, size), jnp.float32)),
        in_specs=[pl.BlockSpec(memory_space=pltpu.SMEM)]
        + [pl.BlockSpec(memory_space=pltpu.VMEM)] * 2,
        out_specs=(pl.BlockSpec(memory_space=pltpu.VMEM),) * 3,
        compiler_params=PARAMS,
        cost_estimate=pl.CostEstimate(
            flops=0, bytes_accessed=32 * size**2, transcendentals=0
        ),
    )(place, own, mate)


def half_kernel(place_ref, band_ref, high_ref, low_ref, *refs):
    edges, parts, (out_ref, top, bottom) = refs[:NX], refs[NX:-3], refs[-3:]
    at = 0
    for upper_ref, lower_ref in zip(parts[::2], parts[1::2]):
        width = upper_ref.shape[1]
        top[:, at : at + width] = upper_ref[...]
        bottom[:, at : at + width] = lower_ref[...]
        at += width

    def fill(ref, mirror):
        for k, edge in enumerate(edges):
            for d in range(4):
                for far in range(2):
                    x, z = (NX - 1 - k, 3 - d) if mirror else (k, d)
                    at = (x * NZ + far * 4 + z) * 16
                    ref[at : at + 16, :] = edge[(d * 2 + far) * 16 : (d * 2 + far + 1) * 16, :]

    @pl.when(place_ref[1] == 0)
    def _():
        fill(top, False)

    @pl.when(place_ref[1] == NX * NZ - 1)
    def _():
        fill(bottom, True)

    dims = (((0,), (0,)), ((), ()))
    total = None
    for m, ref in ((1, band_ref), (0, top), (2, bottom)):
        high, low = split(ref[...])
        for left, block in ((high_ref, low), (low_ref, high), (high_ref, high)):
            part = lax.dot_general(left[m], block, dims, preferred_element_type=jnp.float32)
            total = part if total is None else total + part
    out_ref[...] = total


def half_products(inner, place, covariance, high, low, edges, parts):
    size = covariance.shape[0]
    parts = [piece for part in parts for piece in part]

    def column(rows):
        return pl.BlockSpec((rows, size), lambda i, place: (0, place[0] ^ inner))

    return pl.pallas_call(
        half_kernel,
        out_shape=jax.ShapeDtypeStruct((size, size), jnp.float32),
        grid_spec=pltpu.PrefetchScalarGridSpec(
            num_scalar_prefetch=1,
            grid=(1,),
            in_specs=[column(size)]
            + [whole(3, size, size)] * 2
            + [column(size // NX)] * NX
            + [whole(*piece.shape) for piece in parts],
            out_specs=whole(size, size),
            scratch_shapes=[pltpu.VMEM((size, size), jnp.float32)] * 2,
        ),
        compiler_params=PARAMS,
        cost_estimate=pl.CostEstimate(
            flops=18 * size**3, bytes_accessed=32 * size**2, transcendentals=0
        ),
    )(place, covariance, high, low, *edges, *parts)


def gather_line(right):
    lines = [[x * NZ + z for z in range(NZ)] for x in range(NX)]
    return lax.all_gather(right, "row", axis_index_groups=lines, axis=2, tiled=True)


def gather_ring(line):
    rings = [[x * NZ + z for x in range(NX)] for z in range(NZ)]
    return lax.all_gather(line, "row", axis_index_groups=rings, axis=2, tiled=True)


def outward(x, z, h, y, c):
    return col_step(1 if c == 1 else -1)(x, z, h, y, c)


def toward(distance):
    def target(x, z, h, y, c):
        if z == distance:
            return (x, 0, h, y, c)
        if NZ - 1 - z == distance:
            return (x, NZ - 1, h, y, c)
        return None

    return target


def across(distance):
    def target(x, z, h, y, c):
        if z == 0 and x == distance:
            return (0, z, h, y, c)
        if z == NZ - 1 and NX - 1 - x == distance:
            return (NX - 1, z, h, y, c)
        return None

    return target


def rows_first(edge, z):
    low = z < 4
    keep = jnp.where(low, edge[0], edge[1])
    got = moved(jnp.where(low, edge[1], edge[0]), z_swap(4))
    return jnp.concatenate([jnp.where(low, keep, got), jnp.where(low, got, keep)])


def rows_second(share, gate):
    sent = after(share, *gate)
    return jnp.concatenate([share] + [moved(sent, toward(d)) for d in (1, 2, 3)])


def rows_third(share, gate):
    sent = after(share, *gate)
    return [share] + [moved(sent, across(d)) for d in (1, 2, 3)]


def on_device(covariance, left_ops, right_ops, edge_rows, edge_cols):
    row, col = lax.axis_index("row"), lax.axis_index("col")
    x, z = row // NZ, row % NZ
    h, y, c = col // 8, col // 2 % NY, col % NC
    size = covariance.shape[0]

    def band_of(array, inner):
        return lax.dynamic_slice_in_dim(array, (c ^ inner) * size, size, axis=1)

    line = gather_line(right_ops)
    left = left_ops[0].transpose(0, 2, 1).reshape(96, size)
    pair = left_first(left, edge_cols.transpose(1, 2, 0), h)
    share = rows_first(edge_rows, z)
    band = band_of(covariance, 0)
    outer = [rows_of(band[:, : size // 2])]
    pieces = along_y(after(pair, share, *outer[0]))
    outer.append(rows_of(after(band[:, size // 2 :], share)))
    share = rows_second(share, outer[1])
    right_full = gather_ring(after(line, *outer[1], *pieces))
    pieces = jnp.stack(pieces)
    mates = moved(after(pieces, *outer[1]), core_swap)
    band = after(band_of(covariance, 1), *outer[1])
    inner = [rows_of(band)]
    edges = rows_third(share, outer[0])
    high, low, side = assembled(jnp.stack([h, y, c]), pieces, mates)
    place = jnp.stack([c, row])
    half_outer = half_products(0, place, covariance, high, low, edges, outer)
    cross = moved(half_outer, outward)
    half_inner = half_products(1, place, covariance, high, low, edges, inner)
    sibling = moved(half_inner, core_swap)
    core = jnp.stack([c, jnp.where((col == 0) | (col == 15), 1, 0)])
    return final_products(core, cross, side, half_outer, half_inner, sibling, right_full)


def split(array):
    high = array.astype(jnp.bfloat16)
    return high, (array - high.astype(jnp.float32)).astype(jnp.bfloat16)


def times(a, b):
    dims = (((1,), (1,)), ((), ()))
    total = lax.dot_general(a[0], b[1], dims, preferred_element_type=jnp.float32)
    total += lax.dot_general(a[1], b[0], dims, preferred_element_type=jnp.float32)
    return total + lax.dot_general(a[0], b[0], dims, preferred_element_type=jnp.float32)


def final_kernel(
    c_ref, cross_ref, side_ref, outer_ref, inner_ref, sibling_ref, r0, r1, r2, out_ref, held, high, low
):
    band, part = pl.program_id(0), pl.program_id(1)

    @pl.when((band == 0) & (part == 0))
    def _():
        held[...] = cross_ref[...]

        @pl.when(c_ref[1] == 1)
        def _():
            held[...] = side_ref[...].T

        for k, ref in enumerate((held, outer_ref, inner_ref, sibling_ref)):
            high[k], low[k] = split(ref[...])

    for b, order in ((0, (0, 1, 2)), (1, (3, 2, 1))):

        @pl.when(band == b)
        def _():
            total = None
            for k, ref in zip(order, (r0, r1, r2)):
                product = times((high[k], low[k]), split(ref[...]))
                total = product if total is None else total + product
            out_ref[...] = total


def whole(*shape):
    return pl.BlockSpec(shape, lambda *_: (0,) * len(shape))


PARAMS = pltpu.CompilerParams(vmem_limit_bytes=48 * 2**20)


def final_products(core, cross, side, outer, inner, sibling, right):
    size, parts = outer.shape[0], 2

    def right_at(place):
        def index(band, part, c):
            j = c[0] ^ band
            return (j, place(j), part, 0)

        return pl.BlockSpec((None, None, size // parts, size), index)

    return pl.pallas_call(
        final_kernel,
        out_shape=jax.ShapeDtypeStruct((size, 2 * size), jnp.float32),
        grid_spec=pltpu.PrefetchScalarGridSpec(
            num_scalar_prefetch=1,
            grid=(2, parts),
            in_specs=[whole(size, size)] * 5
            + [right_at(lambda j: 2 * j), right_at(lambda j: 1), right_at(lambda j: 2 - 2 * j)],
            out_specs=pl.BlockSpec(
                (size, size // parts), lambda band, part, c: (0, (c[0] ^ band) * parts + part)
            ),
            scratch_shapes=[pltpu.VMEM((size, size), jnp.float32)]
            + [pltpu.VMEM((4, size, size), jnp.bfloat16)] * 2,
        ),
        compiler_params=PARAMS,
        cost_estimate=pl.CostEstimate(
            flops=36 * size**3, bytes_accessed=52 * size**2, transcendentals=0
        ),
    )(core, cross, side, outer, inner, sibling, right, right, right)


def solution(mesh):
    return jax.shard_map(
        on_device,
        mesh=mesh,
        in_specs=(
            P("row", "col"),
            P("row", None, None, "col"),
            P("col", None, "row", None),
            P(None, "row", "col"),
            P("row", None, "col"),
        ),
        out_specs=P("row", "col"),
        check_vma=False,
    )
```

```python
import jax
import jax.numpy as jnp
from jax import lax
from jax.experimental import pallas as pl
from jax.experimental.pallas import tpu as pltpu
from jax.sharding import PartitionSpec as P

NX, NZ, NH, NY, NC = 4, 8, 2, 4, 2
AXES = ("row", "col")


def moved(array, target):
    pairs = []
    for x in range(NX):
        for z in range(NZ):
            for h in range(NH):
                for y in range(NY):
                    for c in range(NC):
                        to = target(x, z, h, y, c)
                        if to is not None:
                            pairs.append((flat(x, z, h, y, c), flat(*to)))
    return lax.ppermute(array, AXES, pairs)


def flat(x, z, h, y, c):
    return (((x * NZ + z) * NH + h) * NY + y) * NC + c


def row_step(d):
    def target(x, z, h, y, c):
        r = x * NZ + z + d
        return (r // NZ, r % NZ, h, y, c) if 0 <= r < NX * NZ else None

    return target


def col_step(d):
    def target(x, z, h, y, c):
        k = (h * NY + y) * NC + c + d
        return (x, z, k // 8, k % 8 // 2, k % 2) if 0 <= k < 16 else None

    return target


def x_step(d):
    return lambda x, z, h, y, c: ((x + d) % NX, z, h, y, c)


def y_step(d):
    return lambda x, z, h, y, c: (x, z, h, (y + d) % NY, c)


def z_swap(bit):
    return lambda x, z, h, y, c: (x, z ^ bit, h, y, c)


def rows_of(band):
    return moved(band, row_step(1)), moved(band, row_step(-1))


def h_swap(x, z, h, y, c):
    return (x, z, 1 - h, y, c)


def core_swap(x, z, h, y, c):
    return (x, z, h, y, 1 - c)


def after(array, *others):
    return lax.optimization_barrier((array, *others))[0]


def left_first(left, edge, h):
    other = moved(jnp.concatenate([left, jnp.where(h == 0, edge[1], edge[0])], axis=0), h_swap)
    own = jnp.concatenate([left, jnp.where(h == 0, edge[0], edge[1])], axis=0)
    return jnp.stack([own, other])


def along_y(pair):
    return [pair] + [moved(pair, y_step(d)) for d in (-1, 2, 1)]


def assemble_kernel(place_ref, own_ref, mate_ref, high_ref, low_ref, side_ref):
    h, y, c = place_ref[0], place_ref[1], place_ref[2]
    for ref, core in ((own_ref, c), (mate_ref, 1 - c)):
        for d in range(NY):
            line = lax.rem(y + d, NY)
            for far in range(2):
                side = h if far == 0 else 1 - h
                at = pl.multiple_of(((side * NY + line) * NC + core) * 32, 32)
                for m in range(3):
                    high, low = split(ref[d, far, pl.ds(m * 32, 32), :])
                    high_ref[m, pl.ds(at, 32), :] = high
                    low_ref[m, pl.ds(at, 32), :] = low
                side_ref[pl.ds(at, 32), :] = ref[d, far, pl.ds(96, 32), :]


def assembled(place, own, mate):
    size = own.shape[3]
    half = jax.ShapeDtypeStruct((3, size, size), jnp.bfloat16)
    return pl.pallas_call(
        assemble_kernel,
        out_shape=(half, half, jax.ShapeDtypeStruct((size, size), jnp.float32)),
        in_specs=[pl.BlockSpec(memory_space=pltpu.SMEM)]
        + [pl.BlockSpec(memory_space=pltpu.VMEM)] * 2,
        out_specs=(pl.BlockSpec(memory_space=pltpu.VMEM),) * 3,
        compiler_params=PARAMS,
        cost_estimate=pl.CostEstimate(
            flops=0, bytes_accessed=32 * size**2, transcendentals=0
        ),
    )(place, own, mate)


def half_kernel(place_ref, band_ref, high_ref, low_ref, *refs):
    edges, parts, (out_ref, top, bottom) = refs[:NX], refs[NX:-3], refs[-3:]
    at = 0
    for upper_ref, lower_ref in zip(parts[::2], parts[1::2]):
        width = upper_ref.shape[1]
        top[:, at : at + width] = upper_ref[...]
        bottom[:, at : at + width] = lower_ref[...]
        at += width

    def fill(ref, mirror):
        for k, edge in enumerate(edges):
            for d in range(4):
                for far in range(2):
                    x, z = (NX - 1 - k, 3 - d) if mirror else (k, d)
                    at = (x * NZ + far * 4 + z) * 16
                    ref[at : at + 16, :] = edge[(d * 2 + far) * 16 : (d * 2 + far + 1) * 16, :]

    @pl.when(place_ref[1] == 0)
    def _():
        fill(top, False)

    @pl.when(place_ref[1] == NX * NZ - 1)
    def _():
        fill(bottom, True)

    dims = (((0,), (0,)), ((), ()))
    total = None
    for m, ref in ((1, band_ref), (0, top), (2, bottom)):
        high, low = split(ref[...])
        for left, block in ((high_ref, low), (low_ref, high), (high_ref, high)):
            part = lax.dot_general(left[m], block, dims, preferred_element_type=jnp.float32)
            total = part if total is None else total + part
    out_ref[...] = total


def half_products(inner, place, covariance, high, low, edges, parts):
    size = covariance.shape[0]
    parts = [piece for part in parts for piece in part]

    def column(rows):
        return pl.BlockSpec((rows, size), lambda i, place: (0, place[0] ^ inner))

    return pl.pallas_call(
        half_kernel,
        out_shape=jax.ShapeDtypeStruct((size, size), jnp.float32),
        grid_spec=pltpu.PrefetchScalarGridSpec(
            num_scalar_prefetch=1,
            grid=(1,),
            in_specs=[column(size)]
            + [whole(3, size, size)] * 2
            + [column(size // NX)] * NX
            + [whole(*piece.shape) for piece in parts],
            out_specs=whole(size, size),
            scratch_shapes=[pltpu.VMEM((size, size), jnp.float32)] * 2,
        ),
        compiler_params=PARAMS,
        cost_estimate=pl.CostEstimate(
            flops=18 * size**3, bytes_accessed=32 * size**2, transcendentals=0
        ),
    )(place, covariance, high, low, *edges, *parts)


def gather_line(right):
    lines = [[x * NZ + z for z in range(NZ)] for x in range(NX)]
    return lax.all_gather(right, "row", axis_index_groups=lines, axis=2, tiled=True)


def gather_ring(line):
    rings = [[x * NZ + z for x in range(NX)] for z in range(NZ)]
    return lax.all_gather(line, "row", axis_index_groups=rings, axis=2, tiled=True)


def outward(x, z, h, y, c):
    return col_step(1 if c == 1 else -1)(x, z, h, y, c)


def toward(distance):
    def target(x, z, h, y, c):
        if z == distance:
            return (x, 0, h, y, c)
        if NZ - 1 - z == distance:
            return (x, NZ - 1, h, y, c)
        return None

    return target


def across(distance):
    def target(x, z, h, y, c):
        if z == 0 and x == distance:
            return (0, z, h, y, c)
        if z == NZ - 1 and NX - 1 - x == distance:
            return (NX - 1, z, h, y, c)
        return None

    return target


def rows_first(edge, z):
    low = z < 4
    keep = jnp.where(low, edge[0], edge[1])
    got = moved(jnp.where(low, edge[1], edge[0]), z_swap(4))
    return jnp.concatenate([jnp.where(low, keep, got), jnp.where(low, got, keep)])


def rows_second(share, gate):
    sent = after(share, *gate)
    return jnp.concatenate([share] + [moved(sent, toward(d)) for d in (1, 2, 3)])


def rows_third(share, gate):
    sent = after(share, *gate)
    return [share] + [moved(sent, across(d)) for d in (1, 2, 3)]


def on_device(covariance, left_ops, right_ops, edge_rows, edge_cols):
    row, col = lax.axis_index("row"), lax.axis_index("col")
    x, z = row // NZ, row % NZ
    h, y, c = col // 8, col // 2 % NY, col % NC
    size = covariance.shape[0]

    def band_of(array, inner):
        return lax.dynamic_slice_in_dim(array, (c ^ inner) * size, size, axis=1)

    line = gather_line(right_ops)
    left = left_ops[0].transpose(0, 2, 1).reshape(96, size)
    pair = left_first(left, edge_cols.transpose(1, 2, 0), h)
    share = rows_first(edge_rows, z)
    band = band_of(covariance, 0)
    outer = [rows_of(band[:, : size // 2])]
    pieces = along_y(after(pair, share, *outer[0]))
    outer.append(rows_of(after(band[:, size // 2 :], share, pair)))
    share = rows_second(share, outer[1])
    right_full = gather_ring(after(line, *outer[1], *pieces))
    pieces = jnp.stack(pieces)
    mates = moved(after(pieces, *outer[1]), core_swap)
    band = after(band_of(covariance, 1), *outer[1])
    inner = [rows_of(band)]
    edges = rows_third(share, outer[0])
    high, low, side = assembled(jnp.stack([h, y, c]), pieces, mates)
    place = jnp.stack([c, row])
    half_outer = half_products(0, place, covariance, high, low, edges, outer)
    cross = moved(half_outer, outward)
    half_inner = half_products(1, place, covariance, high, low, edges, inner)
    sibling = moved(half_inner, core_swap)
    core = jnp.stack([c, jnp.where((col == 0) | (col == 15), 1, 0)])
    return final_products(core, cross, side, half_outer, half_inner, sibling, right_full)


def split(array):
    high = array.astype(jnp.bfloat16)
    return high, (array - high.astype(jnp.float32)).astype(jnp.bfloat16)


def times(a, b):
    dims = (((1,), (1,)), ((), ()))
    total = lax.dot_general(a[0], b[1], dims, preferred_element_type=jnp.float32)
    total += lax.dot_general(a[1], b[0], dims, preferred_element_type=jnp.float32)
    return total + lax.dot_general(a[0], b[0], dims, preferred_element_type=jnp.float32)


def final_kernel(
    c_ref, cross_ref, side_ref, outer_ref, inner_ref, sibling_ref, r0, r1, r2, out_ref, held, high, low
):
    band, part = pl.program_id(0), pl.program_id(1)

    @pl.when((band == 0) & (part == 0))
    def _():
        held[...] = cross_ref[...]

        @pl.when(c_ref[1] == 1)
        def _():
            held[...] = side_ref[...].T

        for k, ref in enumerate((held, outer_ref, inner_ref, sibling_ref)):
            high[k], low[k] = split(ref[...])

    for b, order in ((0, (0, 1, 2)), (1, (3, 2, 1))):

        @pl.when(band == b)
        def _():
            total = None
            for k, ref in zip(order, (r0, r1, r2)):
                product = times((high[k], low[k]), split(ref[...]))
                total = product if total is None else total + product
            out_ref[...] = total


def whole(*shape):
    return pl.BlockSpec(shape, lambda *_: (0,) * len(shape))


PARAMS = pltpu.CompilerParams(vmem_limit_bytes=48 * 2**20)


def final_products(core, cross, side, outer, inner, sibling, right):
    size, parts = outer.shape[0], 2

    def right_at(place):
        def index(band, part, c):
            j = c[0] ^ band
            return (j, place(j), part, 0)

        return pl.BlockSpec((None, None, size // parts, size), index)

    return pl.pallas_call(
        final_kernel,
        out_shape=jax.ShapeDtypeStruct((size, 2 * size), jnp.float32),
        grid_spec=pltpu.PrefetchScalarGridSpec(
            num_scalar_prefetch=1,
            grid=(2, parts),
            in_specs=[whole(size, size)] * 5
            + [right_at(lambda j: 2 * j), right_at(lambda j: 1), right_at(lambda j: 2 - 2 * j)],
            out_specs=pl.BlockSpec(
                (size, size // parts), lambda band, part, c: (0, (c[0] ^ band) * parts + part)
            ),
            scratch_shapes=[pltpu.VMEM((size, size), jnp.float32)]
            + [pltpu.VMEM((4, size, size), jnp.bfloat16)] * 2,
        ),
        compiler_params=PARAMS,
        cost_estimate=pl.CostEstimate(
            flops=36 * size**3, bytes_accessed=52 * size**2, transcendentals=0
        ),
    )(core, cross, side, outer, inner, sibling, right, right, right)


def solution(mesh):
    return jax.shard_map(
        on_device,
        mesh=mesh,
        in_specs=(
            P("row", "col"),
            P("row", None, None, "col"),
            P("col", None, "row", None),
            P(None, "row", "col"),
            P("row", None, "col"),
        ),
        out_specs=P("row", "col"),
        check_vma=False,
    )
```
